32 devices in a mesh: dp: 8 (over y, x, core), ctx: 4 (over z).
Axes of the slice: x: 2, y: 2, z: 4, core: 2. Of those that a mesh axis runs over, the one named last changes fastest.
Arguments:
- queries: bfloat16 [32768, 8, 128], P(('dp', 'ctx')), parts along dimension 0, may hold values from -6 to 6
- keys: bfloat16 [32768, 128], P(('dp', 'ctx')), parts along dimension 0, may hold values from -6 to 6
- values: bfloat16 [32768, 128], P(('dp', 'ctx')), parts along dimension 0, may hold values from -6 to 6
- output: bfloat16 [32768, 8, 128], P(('dp', 'ctx')), parts along dimension 0, may hold values from -6 to 6
- d_output: bfloat16 [32768, 8, 128], P(('dp', 'ctx')), parts along dimension 0, may hold values from -6 to 6
- block_lists: int32 [128, 3], P('dp'), parts along dimension 0, may hold values from -1 to 15, as said below
Outputs:
- d_queries: bfloat16 [32768, 8, 128], P(('dp', 'ctx')), parts along dimension 0
- d_keys: bfloat16 [32768, 128], P(('dp', 'ctx')), parts along dimension 0
- d_values: bfloat16 [32768, 128], P(('dp', 'ctx')), parts along dimension 0
The draws below stay inside these ranges and needn't reach their ends.
There are 8 independent parts, one for each index of `dp`. The reference program is written for one: setup_inputs(seed, part) draws one part's arguments, and reference() takes and returns one part's arrays. A program takes and returns all parts, laid end to end along the dimension named above; each array names one. Nothing has to cross between parts.
Inputs may be any that keep to these rules, and one draw needn't show every extreme that they name: `block_lists`: row b: entry 0 is b itself; the other 2 entries are distinct blocks below b, or -1 where fewer than 2 blocks lie below b.
All inputs are finite; a program needn't handle non-finite values.
Results may differ from the reference program's by a relative error of at most 0.005.
Values may be sent and summed in bfloat16 or wider, within the bound.
A program may use at most 192 MiB of HBM per device.

```python
import jax
import jax.numpy as jnp
from jax import lax

HQ = 8
HD = 128
BLK = 256
TOPK = 3
TOKENS = 4096


def draw_queries(key, part):
    drawn = jnp.clip(jax.random.normal(jax.random.fold_in(key, 3), (TOKENS, HQ, HD), jnp.float32), -6.0, 6.0)
    return drawn.astype(jnp.bfloat16)


def draw_keys(key, part):
    drawn = jnp.clip(jax.random.normal(jax.random.fold_in(key, 4), (TOKENS, HD), jnp.float32), -6.0, 6.0)
    return drawn.astype(jnp.bfloat16)


def draw_block_lists(key, part):
    nblocks = TOKENS // BLK
    jitter_draw = jax.random.randint(jax.random.fold_in(key, 21), (nblocks, nblocks), 0, 64)
    favour = jax.random.randint(jax.random.fold_in(key, 22), (nblocks,), 0, 4)
    column = jnp.arange(nblocks, dtype=jnp.int32)
    ranking = ((jitter_draw + 64 * favour[None, :]) * nblocks + column[None, :]).astype(jnp.int32)
    earlier = column[None, :] < column[:, None]
    ranking = jnp.where(earlier, ranking, -1)
    top_values, top_index = lax.top_k(ranking, TOPK - 1)
    chosen = jnp.where(top_values >= 0, top_index, -1)
    return jnp.concatenate([column[:, None], chosen], axis=1).astype(jnp.int32)


def shard_levels(stream_key, extent, shards, least, top_value):
    def one(axis_at, blocks):
        steps = jax.random.uniform(jax.random.fold_in(jax.random.fold_in(stream_key, 6), axis_at), (blocks,), jnp.float32, least / len(shards), top_value / len(shards))
        return jnp.repeat(jnp.exp(steps), extent[axis_at] // blocks).reshape((-1,) + (1,) * (len(extent) - axis_at - 1))

    level = one(*shards[0])
    for cut in shards[1:]:
        level = level * one(*cut)
    return level


def centred(own_key, dims, scale, reach, cuts=(), kind=jnp.bfloat16):
    entries = jax.random.normal(own_key, dims, jnp.float32) * scale
    if len(cuts) > 0:
        entries = shard_levels(own_key, dims, cuts, -0.22, 0.18) * entries
    return jnp.clip(entries, min=-reach, max=reach).astype(kind)


def setup_inputs(seed: int = 0, part: int = 0) -> dict:
    key_list = jax.random.split(jax.random.key(seed), 7)
    part_splits = jax.random.split(jax.random.fold_in(key_list[6], part), 7)
    queries = draw_queries(jax.random.fold_in(jax.random.fold_in(key_list[6], part), 71), part)
    keys = draw_keys(jax.random.fold_in(jax.random.fold_in(key_list[6], part), 71), part)
    values = centred(part_splits[2], (TOKENS, HD), 1.0, 6.0, ((0, 4),))
    output = centred(part_splits[3], (TOKENS, HQ, HD), 1.0, 6.0, ((0, 4),))
    d_output = centred(part_splits[4], (TOKENS, HQ, HD), 1.0, 6.0, ((0, 4),))
    block_lists = draw_block_lists(jax.random.fold_in(jax.random.fold_in(key_list[6], part), 71), part)
    return {"queries": queries, "keys": keys, "values": values, "output": output, "d_output": d_output, "block_lists": block_lists}


def reference(queries, keys, values, output, d_output, block_lists):
    nblocks = TOKENS // BLK
    scaling = HD ** -0.5
    query_f = queries.astype(jnp.float32).reshape(nblocks, BLK, HQ, HD)
    output_f = output.astype(jnp.float32).reshape(nblocks, BLK, HQ, HD)
    grad_f = d_output.astype(jnp.float32).reshape(nblocks, BLK, HQ, HD)
    key_f = keys.astype(jnp.float32)
    value_f = values.astype(jnp.float32)

    def one_block(carried, inputs):
        key_grad, value_grad = carried
        block_index, chosen, q_block, o_block, g_block = inputs
        starts = (jnp.maximum(chosen, 0) * BLK).astype(jnp.int32)
        key_sel = jnp.stack([lax.dynamic_slice_in_dim(key_f, starts[slot_index], BLK, 0) for slot_index in range(TOPK)])
        value_sel = jnp.stack([lax.dynamic_slice_in_dim(value_f, starts[slot_index], BLK, 0) for slot_index in range(TOPK)])
        raw = jnp.einsum("qhd,tkd->hqtk", q_block, key_sel) * scaling
        key_pos = starts[:, None] + jnp.arange(BLK, dtype=jnp.int32)[None, :]
        query_pos = (block_index * BLK + jnp.arange(BLK, dtype=jnp.int32)).astype(jnp.int32)
        allowed = (chosen >= 0)[None, :, None] & (key_pos[None, :, :] <= query_pos[:, None, None])
        scores = jnp.where(allowed[None], raw, -jnp.inf)
        top = jnp.max(scores, axis=(2, 3), keepdims=True)
        exps = jnp.exp(scores - top)
        prob = exps / jnp.sum(exps, axis=(2, 3), keepdims=True)
        prob_rounded = lax.optimization_barrier(prob.astype(jnp.bfloat16)).astype(jnp.float32)
        d_prob = jnp.einsum("qhd,tkd->hqtk", g_block, value_sel)
        delta = jnp.transpose(jnp.sum(g_block * o_block, axis=2))[:, :, None, None]
        d_scores = lax.optimization_barrier((prob * (d_prob - delta)).astype(jnp.bfloat16)).astype(jnp.float32)
        d_query = (jnp.einsum("hqtk,tkd->qhd", d_scores, key_sel) * scaling).astype(jnp.bfloat16)
        key_parts = jnp.einsum("hqtk,qhd->tkd", d_scores, q_block) * scaling
        value_parts = jnp.einsum("hqtk,qhd->tkd", prob_rounded, g_block)
        for slot_index in range(TOPK):
            begin = starts[slot_index]
            key_grad = lax.dynamic_update_slice_in_dim(key_grad, lax.dynamic_slice_in_dim(key_grad, begin, BLK, 0) + key_parts[slot_index], begin, 0)
            value_grad = lax.dynamic_update_slice_in_dim(value_grad, lax.dynamic_slice_in_dim(value_grad, begin, BLK, 0) + value_parts[slot_index], begin, 0)
        return (key_grad, value_grad), d_query

    zeros_grad = jnp.zeros((TOKENS, HD), jnp.float32)
    indices = jnp.arange(nblocks, dtype=jnp.int32)
    (key_grad, value_grad), d_query = lax.scan(one_block, (zeros_grad, zeros_grad), (indices, block_lists, query_f, output_f, grad_f))
    return d_query.reshape(TOKENS, HQ, HD), key_grad.astype(jnp.bfloat16), value_grad.astype(jnp.bfloat16)
```

```python
import functools

import jax
import jax.numpy as jnp
from jax import lax
from jax.experimental import pallas as pl
from jax.experimental.pallas import tpu as pltpu
from jax.sharding import PartitionSpec as P

BLK = 256
TOPK = 3
CH = 256
MESH = pl.DeviceIdType.MESH
LOG2E = 1.4426950408889634


def kernel(
    n, nb, heads, hd,
    lists, q_hbm, k_hbm, v_hbm, o_hbm, g_hbm,
    dq_hbm, dk_hbm, dv_hbm,
    q, g, o, qt, gt, delta, probs, kfull, vfull, kcat, kcat_t, vcat,
    part_v, part_k, dvbuf, dkbuf,
    in_sem, out_sem, own_sem,
    k_send, k_recv, v_send, v_recv, dv_send, dv_recv, dk_send, dk_recv,
):
    me = lax.axis_index("ctx")
    rows = BLK * heads
    nch = rows // CH
    scaling = hd ** (-0.5)
    last = n - 1

    def up(hbm, full, send, recv, owner, own):
        src = hbm if own else full.at[pl.ds(owner * nb, nb)]
        return pltpu.make_async_remote_copy(
            src_ref=src,
            dst_ref=full.at[pl.ds(owner * nb, nb)],
            send_sem=send.at[owner],
            recv_sem=recv.at[owner],
            device_id={"ctx": me + 1},
            device_id_type=MESH,
        )

    k_up = functools.partial(up, k_hbm, kfull, k_send, k_recv)
    v_up = functools.partial(up, v_hbm, vfull, v_send, v_recv)

    def down(buf, send, recv, owner):
        return pltpu.make_async_remote_copy(
            src_ref=buf.at[owner],
            dst_ref=buf.at[owner],
            send_sem=send.at[owner],
            recv_sem=recv.at[owner],
            device_id={"ctx": me - 1},
            device_id_type=MESH,
        )

    dv_down = functools.partial(down, dvbuf, dv_send, dv_recv)
    dk_down = functools.partial(down, dkbuf, dk_send, dk_recv)

    def in_copy(lb, which):
        src, dst = ((q_hbm, q), (g_hbm, g), (o_hbm, o))[which]
        return pltpu.make_async_copy(src.at[lb], dst.at[lb], in_sem.at[which, lb])

    def dq_copy(lb):
        return pltpu.make_async_copy(o.at[lb], dq_hbm.at[lb], out_sem.at[lb])

    own_k = pltpu.make_async_copy(k_hbm, kfull.at[pl.ds(me * nb, nb)], own_sem.at[0])
    own_v = pltpu.make_async_copy(v_hbm, vfull.at[pl.ds(me * nb, nb)], own_sem.at[1])

    barrier = pltpu.get_barrier_semaphore()

    @pl.when(me > 0)
    def _():
        pl.semaphore_signal(barrier, inc=1, device_id={"ctx": me - 1}, device_id_type=MESH)

    @pl.when(me < last)
    def _():
        pl.semaphore_signal(barrier, inc=1, device_id={"ctx": me + 1}, device_id_type=MESH)

    pl.semaphore_wait(barrier, jnp.where(me > 0, 1, 0) + jnp.where(me < last, 1, 0))

    @pl.when(me < last)
    def _():
        k_up(me, True).start()

    own_k.start()
    for lb in range(nb):
        for which in range(3):
            in_copy(lb, which).start()
    own_v.start()

    def prep(lb):
        for which in range(3):
            in_copy(lb, which).wait()

        def chunk(ci, _):
            span = pl.ds(ci * CH, CH)
            gc = g[lb, span]
            qt[lb, ci] = q[lb, span].T
            gt[lb, ci] = gc.T
            prod = gc.astype(jnp.float32) * o[lb, span].astype(jnp.float32)
            delta[lb, ci] = jnp.sum(prod.T, axis=0, keepdims=True)
            return 0

        lax.fori_loop(0, nch, chunk, 0)
        part_v[lb, TOPK] = jnp.zeros((BLK, hd), jnp.float32)
        part_k[lb, TOPK] = jnp.zeros((BLK, hd), jnp.float32)

    def pass_key(j):
        @pl.when(me >= j)
        def _():
            k_up(me - j, False).wait_recv()

            @pl.when(me < last)
            def _():
                k_up(me - j, False).start()

    done = 0
    for j in range(1, n):
        if done < nb:
            prep(done)
            done += 1
        pass_key(j)

    @pl.when(me < last)
    def _():
        v_up(me, True).start()

    for lb in range(done, nb):
        prep(lb)
    own_k.wait()

    def pass_value(j):
        @pl.when((me >= j) & (me < last))
        def _():
            v_up(me - j, False).wait_recv()
            v_up(me - j, False).start()

    def entry(lb, t):
        return lists[me * nb + lb, t]

    def phase_a(lb):
        kcat[0:BLK] = kfull[me * nb + lb]
        for t in range(1, TOPK):
            kcat[t * BLK : (t + 1) * BLK] = kfull[jnp.maximum(entry(lb, t), 0)]
        for t in range(TOPK):
            part_v[lb, t] = jnp.zeros((BLK, hd), jnp.float32)
        listed = [entry(lb, t) >= 0 for t in range(1, TOPK)]

        def chunk(ci, _):
            raw = jnp.dot(kcat[...], qt[lb, ci], preferred_element_type=jnp.float32)
            key = lax.broadcasted_iota(jnp.int32, (BLK, CH), 0)
            row = lax.broadcasted_iota(jnp.int32, (BLK, CH), 1) + ci * CH
            pieces = [jnp.where(key * heads <= row, raw[:BLK], -jnp.inf)]
            for t in range(1, TOPK):
                pieces.append(raw[t * BLK : (t + 1) * BLK])
            top = jnp.max(pieces[0], axis=0, keepdims=True)
            for t in range(1, TOPK):
                high = jnp.max(pieces[t], axis=0, keepdims=True)
                top = jnp.maximum(top, jnp.where(listed[t - 1], high, -jnp.inf))
            exps = []
            total = jnp.zeros((1, CH), jnp.float32)
            for t in range(TOPK):
                low = top if t == 0 else jnp.where(listed[t - 1], top, jnp.inf)
                e = jnp.exp2((pieces[t] - low) * (scaling * LOG2E))
                total = total + jnp.sum(e, axis=0, keepdims=True)
                exps.append(e)
            inv = 1.0 / total
            gc = g[lb, pl.ds(ci * CH, CH)]
            for t in range(TOPK):
                p = exps[t] * inv
                probs[lb, ci, t * BLK : (t + 1) * BLK] = p
                part_v[lb, t] += jnp.dot(
                    p.astype(jnp.bfloat16), gc, preferred_element_type=jnp.float32
                )
            return 0

        lax.fori_loop(0, nch, chunk, 0)

    def phase_b(lb):
        kcat[0:BLK] = kfull[me * nb + lb]
        vcat[0:BLK] = vfull[me * nb + lb]
        for t in range(1, TOPK):
            block = jnp.maximum(entry(lb, t), 0)
            kcat[t * BLK : (t + 1) * BLK] = kfull[block]
            vcat[t * BLK : (t + 1) * BLK] = vfull[block]
        kcat_t[...] = kcat[...].T
        for t in range(TOPK):
            part_k[lb, t] = jnp.zeros((BLK, hd), jnp.float32)

        def chunk(ci, _):
            span = pl.ds(ci * CH, CH)
            d_prob = jnp.dot(vcat[...], gt[lb, ci], preferred_element_type=jnp.float32)
            ds = (probs[lb, ci] * (d_prob - delta[lb, ci])).astype(jnp.bfloat16)
            qc = q[lb, span]
            for t in range(TOPK):
                part_k[lb, t] += jnp.dot(
                    ds[t * BLK : (t + 1) * BLK], qc, preferred_element_type=jnp.float32
                )
            dq_t = jnp.dot(kcat_t[...], ds, preferred_element_type=jnp.float32)
            o[lb, span] = (dq_t.T * scaling).astype(jnp.bfloat16)
            return 0

        lax.fori_loop(0, nch, chunk, 0)
        dq_copy(lb).start()

    def local_sum(part, block):
        total = None
        for lb in range(nb):
            slot = jnp.int32(TOPK)
            for t in range(TOPK):
                slot = jnp.where(entry(lb, t) == block, t, slot)
            term = part[lb, slot]
            total = term if total is None else total + term
        return total

    def chain(part, buf, copy, factor, owner):
        @pl.when(owner <= me)
        def _():
            @pl.when(me < last)
            def _():
                copy(owner).wait_recv()

                def add(i, _):
                    total = local_sum(part, owner * nb + i) + buf[owner, i].astype(jnp.float32)
                    buf[owner, i] = (total * jnp.where(owner == me, factor, 1.0)).astype(jnp.bfloat16)
                    return 0

                lax.fori_loop(0, nb, add, 0)

            @pl.when(me == last)
            def _():
                def add(i, _):
                    total = local_sum(part, owner * nb + i)
                    buf[owner, i] = (total * jnp.where(owner == me, factor, 1.0)).astype(jnp.bfloat16)
                    return 0

                lax.fori_loop(0, nb, add, 0)

            @pl.when(owner < me)
            def _():
                copy(owner).start()

    def dv_step(owner):
        chain(part_v, dvbuf, dv_down, 1.0, owner)

    def dk_step(owner):
        chain(part_k, dkbuf, dk_down, scaling, owner)

    def loop(low, high, step):
        def body(i, _):
            step(i)
            return 0

        if low < high:
            lax.fori_loop(low, high, body, 0)

    late = nb - 2
    loop(0, late + 1, phase_a)
    pass_value(1)
    loop(late + 1, nb, phase_a)
    loop(2, n, pass_value)

    @pl.when(me == last)
    def _():
        loop(0, n, dv_step)

        def arrive(j, _):
            v_up(me - j, False).wait_recv()
            return 0

        lax.fori_loop(1, n, arrive, 0)

    own_v.wait()

    half = nb // 2
    loop(0, half, phase_b)

    @pl.when(me < last)
    def _():
        dv_step(0)

    loop(half, nb, phase_b)

    @pl.when(me < last)
    def _():
        loop(1, n, dv_step)

    dv_out = pltpu.make_async_copy(dvbuf.at[me], dv_hbm, own_sem.at[1])
    dv_out.start()
    loop(0, n, dk_step)
    dk_out = pltpu.make_async_copy(dkbuf.at[me], dk_hbm, own_sem.at[0])
    dk_out.start()
    for lb in range(nb):
        dq_copy(lb).wait()

    def finish_up(j, _):
        @pl.when(j <= me)
        def _():
            @pl.when(me < last)
            def _():
                k_up(j, False).wait_send()
                v_up(j, False).wait_send()

        @pl.when(j < me)
        def _():
            dv_down(j).wait_send()
            dk_down(j).wait_send()

        return 0

    lax.fori_loop(0, n, finish_up, 0)
    dv_out.wait()
    dk_out.wait()


def shards(queries, keys, values, output, d_output, block_lists):
    tokens, heads, hd = queries.shape
    n = lax.axis_size("ctx")
    nb = tokens // BLK
    rows = BLK * heads
    nch = rows // CH
    flat = (nb, rows, hd)
    blocks = (nb, BLK, hd)
    bf16, f32 = jnp.bfloat16, jnp.float32
    dma = pltpu.SemaphoreType.DMA
    any_spec = pl.BlockSpec(memory_space=pl.ANY)
    pairs = nb * TOPK
    d_queries, d_keys, d_values = pl.pallas_call(
        functools.partial(kernel, n, nb, heads, hd),
        out_shape=(
            jax.ShapeDtypeStruct(flat, bf16),
            jax.ShapeDtypeStruct(blocks, bf16),
            jax.ShapeDtypeStruct(blocks, bf16),
        ),
        in_specs=[pl.BlockSpec(memory_space=pltpu.SMEM)] + [any_spec] * 5,
        out_specs=(any_spec,) * 3,
        scratch_shapes=[
            pltpu.VMEM(flat, bf16),
            pltpu.VMEM(flat, bf16),
            pltpu.VMEM(flat, bf16),
            pltpu.VMEM((nb, nch, hd, CH), bf16),
            pltpu.VMEM((nb, nch, hd, CH), bf16),
            pltpu.VMEM((nb, nch, 1, CH), f32),
            pltpu.VMEM((nb, nch, TOPK * BLK, CH), f32),
            pltpu.VMEM((n * nb, BLK, hd), bf16),
            pltpu.VMEM((n * nb, BLK, hd), bf16),
            pltpu.VMEM((TOPK * BLK, hd), bf16),
            pltpu.VMEM((hd, TOPK * BLK), bf16),
            pltpu.VMEM((TOPK * BLK, hd), bf16),
            pltpu.VMEM((nb, TOPK + 1, BLK, hd), f32),
            pltpu.VMEM((nb, TOPK + 1, BLK, hd), f32),
            pltpu.VMEM((n, nb, BLK, hd), bf16),
            pltpu.VMEM((n, nb, BLK, hd), bf16),
            dma((3, nb)),
            dma((nb,)),
            dma((2,)),
        ]
        + [dma((n,))] * 8,
        compiler_params=pltpu.CompilerParams(
            collective_id=0, has_side_effects=True, vmem_limit_bytes=63 * 1024 * 1024
        ),
        cost_estimate=pl.CostEstimate(
            flops=pairs * 5 * 2 * rows * BLK * hd,
            bytes_accessed=4 * tokens * heads * hd * 2 + 4 * tokens * hd * 2,
            transcendentals=pairs * rows * BLK,
        ),
    )(
        block_lists,
        queries.reshape(flat),
        keys.reshape(blocks),
        values.reshape(blocks),
        output.reshape(flat),
        d_output.reshape(flat),
    )
    return (
        d_queries.reshape(queries.shape),
        d_keys.reshape(keys.shape),
        d_values.reshape(values.shape),
    )


def solution(mesh):
    return jax.shard_map(
        shards,
        mesh=mesh,
        in_specs=(
            P(("dp", "ctx"), None, None),
            P(("dp", "ctx"), None),
            P(("dp", "ctx"), None),
            P(("dp", "ctx"), None, None),
            P(("dp", "ctx"), None, None),
            P("dp", None),
        ),
        out_specs=(P(("dp", "ctx"), None, None), P(("dp", "ctx"), None), P(("dp", "ctx"), None)),
        check_vma=False,
    )
```

```python
import functools

import jax
import jax.numpy as jnp
from jax import lax
from jax.experimental import pallas as pl
from jax.experimental.pallas import tpu as pltpu
from jax.sharding import PartitionSpec as P

BLK = 256
TOPK = 3
CH = 256
MESH = pl.DeviceIdType.MESH
LOG2E = 1.4426950408889634


def kernel(
    n, nb, heads, hd,
    lists, q_hbm, k_hbm, v_hbm, o_hbm, g_hbm,
    dq_hbm, dk_hbm, dv_hbm,
    q, g, o, qt, gt, delta, top0, sum0, fac0, probs, kfull, vfull, kcat, kcat_t, vcat,
    part_v, part_k, dvbuf, dkbuf,
    in_sem, out_sem, own_sem,
    k_send, k_recv, v_send, v_recv, dv_send, dv_recv, dk_send, dk_recv,
):
    me = lax.axis_index("ctx")
    rows = BLK * heads
    nch = rows // CH
    scaling = hd ** (-0.5)
    last = n - 1

    def up(hbm, full, send, recv, owner, i, own):
        at = owner * nb + i
        return pltpu.make_async_remote_copy(
            src_ref=hbm.at[i] if own else full.at[at],
            dst_ref=full.at[at],
            send_sem=send.at[at],
            recv_sem=recv.at[at],
            device_id={"ctx": me + 1},
            device_id_type=MESH,
        )

    k_up = functools.partial(up, k_hbm, kfull, k_send, k_recv)
    v_up = functools.partial(up, v_hbm, vfull, v_send, v_recv)

    def down(buf, send, recv, at):
        return pltpu.make_async_remote_copy(
            src_ref=buf.at[at],
            dst_ref=buf.at[at],
            send_sem=send.at[at],
            recv_sem=recv.at[at],
            device_id={"ctx": me - 1},
            device_id_type=MESH,
        )

    dv_down = functools.partial(down, dvbuf, dv_send, dv_recv)
    dk_down = functools.partial(down, dkbuf, dk_send, dk_recv)

    def loop(low, high, step):
        def body(i, _):
            step(i)
            return 0

        if low < high:
            lax.fori_loop(low, high, body, 0)

    def in_copy(lb, which):
        src, dst = ((q_hbm, q), (g_hbm, g), (o_hbm, o))[which]
        return pltpu.make_async_copy(src.at[lb], dst.at[lb], in_sem.at[which, lb])

    def dq_copy(lb):
        return pltpu.make_async_copy(o.at[lb], dq_hbm.at[lb], out_sem.at[lb])

    own_k = pltpu.make_async_copy(k_hbm, kfull.at[pl.ds(me * nb, nb)], own_sem.at[0])
    own_v = pltpu.make_async_copy(v_hbm, vfull.at[pl.ds(me * nb, nb)], own_sem.at[1])

    barrier = pltpu.get_barrier_semaphore()

    @pl.when(me > 0)
    def _():
        pl.semaphore_signal(barrier, inc=1, device_id={"ctx": me - 1}, device_id_type=MESH)

    @pl.when(me < last)
    def _():
        pl.semaphore_signal(barrier, inc=1, device_id={"ctx": me + 1}, device_id_type=MESH)

    pl.semaphore_wait(barrier, jnp.where(me > 0, 1, 0) + jnp.where(me < last, 1, 0))

    @pl.when(me < last)
    def _():
        for i in range(nb):
            k_up(me, i, True).start()

    own_k.start()
    for lb in range(nb):
        for which in range(3):
            in_copy(lb, which).start()
    own_v.start()
    own_k.wait()

    def prep(lb):
        for which in range(3):
            in_copy(lb, which).wait()

        def chunk(ci, _):
            span = pl.ds(ci * CH, CH)
            gc = g[lb, span]
            qc_t = q[lb, span].T
            qt[lb, ci] = qc_t
            gt[lb, ci] = gc.T
            prod = gc.astype(jnp.float32) * o[lb, span].astype(jnp.float32)
            delta[lb, ci] = jnp.sum(prod.T, axis=0, keepdims=True)
            raw = jnp.dot(kfull[me * nb + lb], qc_t, preferred_element_type=jnp.float32)
            key = lax.broadcasted_iota(jnp.int32, (BLK, CH), 0)
            row = lax.broadcasted_iota(jnp.int32, (BLK, CH), 1) + ci * CH
            raw = jnp.where(key * heads <= row, raw, -jnp.inf)
            top = jnp.max(raw, axis=0, keepdims=True)
            e = jnp.exp2((raw - top) * (scaling * LOG2E))
            probs[lb, ci, 0:BLK] = e
            top0[lb, ci] = top
            sum0[lb, ci] = jnp.sum(e, axis=0, keepdims=True)
            return 0

        lax.fori_loop(0, nch, chunk, 0, unroll=2)
        part_v[lb, TOPK] = jnp.zeros((BLK, hd), jnp.float32)
        part_k[lb, TOPK] = jnp.zeros((BLK, hd), jnp.float32)

    def pass_key(j):
        @pl.when(me >= j)
        def _():
            def one(i):
                k_up(me - j, i, False).wait_recv()

                @pl.when(me < last)
                def _():
                    k_up(me - j, i, False).start()

            loop(0, nb, one)

    loop(0, 2, prep)
    pass_key(1)
    loop(2, nb, prep)
    loop(2, n, pass_key)

    @pl.when(me < last)
    def _():
        for i in range(nb):
            v_up(me, i, True).start()

    def pass_value(j):
        @pl.when((me >= j) & (me < last))
        def _():
            def one(i):
                v_up(me - j, i, False).wait_recv()
                v_up(me - j, i, False).start()

            loop(0, nb, one)

    def entry(lb, t):
        return lists[me * nb + lb, t]

    def phase_a(lb):
        for t in range(1, TOPK):
            kcat[t * BLK : (t + 1) * BLK] = kfull[jnp.maximum(entry(lb, t), 0)]
            part_v[lb, t] = jnp.zeros((BLK, hd), jnp.float32)
        listed = [entry(lb, t) >= 0 for t in range(1, TOPK)]

        def chunk(ci, _):
            raw = jnp.dot(kcat[BLK:], qt[lb, ci], preferred_element_type=jnp.float32)
            first = top0[lb, ci]
            top = first
            for t in range(TOPK - 1):
                high = jnp.max(raw[t * BLK : (t + 1) * BLK], axis=0, keepdims=True)
                top = jnp.maximum(top, jnp.where(listed[t], high, -jnp.inf))
            shrink = jnp.exp2((first - top) * (scaling * LOG2E))
            total = sum0[lb, ci] * shrink
            exps = []
            for t in range(TOPK - 1):
                low = jnp.where(listed[t], top, jnp.inf)
                e = jnp.exp2((raw[t * BLK : (t + 1) * BLK] - low) * (scaling * LOG2E))
                total = total + jnp.sum(e, axis=0, keepdims=True)
                exps.append(e)
            inv = 1.0 / total
            fac0[lb, ci] = shrink * inv
            gc = g[lb, pl.ds(ci * CH, CH)]
            for t in range(1, TOPK):
                p = exps[t - 1] * inv
                probs[lb, ci, t * BLK : (t + 1) * BLK] = p
                part_v[lb, t] += jnp.dot(
                    p.astype(jnp.bfloat16), gc, preferred_element_type=jnp.float32
                )
            return 0

        lax.fori_loop(0, nch, chunk, 0, unroll=2)

    def phase_b(lb):
        kcat[0:BLK] = kfull[me * nb + lb]
        vcat[0:BLK] = vfull[me * nb + lb]
        for t in range(1, TOPK):
            block = jnp.maximum(entry(lb, t), 0)
            kcat[t * BLK : (t + 1) * BLK] = kfull[block]
            vcat[t * BLK : (t + 1) * BLK] = vfull[block]
        kcat_t[...] = kcat[...].T
        for t in range(TOPK):
            part_k[lb, t] = jnp.zeros((BLK, hd), jnp.float32)
        part_v[lb, 0] = jnp.zeros((BLK, hd), jnp.float32)

        def chunk(ci, _):
            span = pl.ds(ci * CH, CH)
            d_prob = jnp.dot(vcat[...], gt[lb, ci], preferred_element_type=jnp.float32)
            qc = q[lb, span]
            dq_t = jnp.zeros((hd, CH), jnp.float32)
            for t in range(TOPK):
                part = slice(t * BLK, (t + 1) * BLK)
                p = probs[lb, ci, part]
                if t == 0:
                    p = p * fac0[lb, ci]
                    part_v[lb, 0] += jnp.dot(
                        p.astype(jnp.bfloat16), g[lb, span], preferred_element_type=jnp.float32
                    )
                ds = (p * (d_prob[part] - delta[lb, ci])).astype(jnp.bfloat16)
                part_k[lb, t] += jnp.dot(ds, qc, preferred_element_type=jnp.float32)
                dq_t = dq_t + jnp.dot(kcat_t[:, part], ds, preferred_element_type=jnp.float32)
            o[lb, span] = (dq_t.T * scaling).astype(jnp.bfloat16)
            return 0

        lax.fori_loop(0, nch, chunk, 0, unroll=2)
        dq_copy(lb).start()

    def local_sum(part, block):
        total = None
        for lb in range(nb):
            slot = jnp.int32(TOPK)
            for t in range(TOPK):
                slot = jnp.where(entry(lb, t) == block, t, slot)
            term = part[lb, slot]
            total = term if total is None else total + term
        return total

    def chain(part, buf, copy, factor, owner):
        def one(i):
            at = owner * nb + i

            def put(total):
                buf[at] = (total * jnp.where(owner == me, factor, 1.0)).astype(jnp.bfloat16)

            @pl.when(me < last)
            def _():
                copy(at).wait_recv()
                put(local_sum(part, at) + buf[at].astype(jnp.float32))

            @pl.when(me == last)
            def _():
                put(local_sum(part, at))

            @pl.when(owner < me)
            def _():
                copy(at).start()

        @pl.when(owner <= me)
        def _():
            loop(0, nb, one)

    def dv_step(owner):
        chain(part_v, dvbuf, dv_down, 1.0, owner)

    def dk_step(owner):
        chain(part_k, dkbuf, dk_down, scaling, owner)

    late = nb - 2
    loop(0, late, phase_a)
    pass_value(1)
    loop(late, nb - 1, phase_a)
    if n > 2:
        pass_value(2)
    phase_a(nb - 1)
    loop(3, n, pass_value)

    @pl.when(me == last)
    def _():
        loop(0, n - 1, dv_step)

        def arrive(j):
            loop(0, nb, lambda i: v_up(me - j, i, False).wait_recv())

        loop(1, n, arrive)

    own_v.wait()

    half = nb // 2
    loop(0, half, phase_b)

    @pl.when((me > 0) & (me < last))
    def _():
        dv_step(0)

    loop(half, nb, phase_b)

    @pl.when(me == 0)
    def _():
        dv_step(0)

    @pl.when((me > 0) & (me < last))
    def _():
        loop(1, n, dv_step)

    @pl.when(me == last)
    def _():
        loop(0, n, dk_step)
        dv_step(last)

    dv_out = pltpu.make_async_copy(dvbuf.at[pl.ds(me * nb, nb)], dv_hbm, own_sem.at[1])
    dv_out.start()

    @pl.when(me < last)
    def _():
        loop(0, n, dk_step)

    dk_out = pltpu.make_async_copy(dkbuf.at[pl.ds(me * nb, nb)], dk_hbm, own_sem.at[0])
    dk_out.start()
    for lb in range(nb):
        dq_copy(lb).wait()

    def finish_up(j):
        def one(i):
            @pl.when((j <= me) & (me < last))
            def _():
                k_up(j, i, False).wait_send()
                v_up(j, i, False).wait_send()

            @pl.when(j < me)
            def _():
                dv_down(j * nb + i).wait_send()
                dk_down(j * nb + i).wait_send()

        loop(0, nb, one)

    loop(0, n, finish_up)
    dv_out.wait()
    dk_out.wait()


def shards(queries, keys, values, output, d_output, block_lists):
    tokens, heads, hd = queries.shape
    n = lax.axis_size("ctx")
    nb = tokens // BLK
    rows = BLK * heads
    nch = rows // CH
    flat = (nb, rows, hd)
    blocks = (nb, BLK, hd)
    bf16, f32 = jnp.bfloat16, jnp.float32
    dma = pltpu.SemaphoreType.DMA
    any_spec = pl.BlockSpec(memory_space=pl.ANY)
    pairs = nb * TOPK
    d_queries, d_keys, d_values = pl.pallas_call(
        functools.partial(kernel, n, nb, heads, hd),
        out_shape=(
            jax.ShapeDtypeStruct(flat, bf16),
            jax.ShapeDtypeStruct(blocks, bf16),
            jax.ShapeDtypeStruct(blocks, bf16),
        ),
        in_specs=[pl.BlockSpec(memory_space=pltpu.SMEM)] + [any_spec] * 5,
        out_specs=(any_spec,) * 3,
        scratch_shapes=[
            pltpu.VMEM(flat, bf16),
            pltpu.VMEM(flat, bf16),
            pltpu.VMEM(flat, bf16),
            pltpu.VMEM((nb, nch, hd, CH), bf16),
            pltpu.VMEM((nb, nch, hd, CH), bf16),
            pltpu.VMEM((nb, nch, 1, CH), f32),
            pltpu.VMEM((nb, nch, 1, CH), f32),
            pltpu.VMEM((nb, nch, 1, CH), f32),
            pltpu.VMEM((nb, nch, 1, CH), f32),
            pltpu.VMEM((nb, nch, TOPK * BLK, CH), f32),
            pltpu.VMEM((n * nb, BLK, hd), bf16),
            pltpu.VMEM((n * nb, BLK, hd), bf16),
            pltpu.VMEM((TOPK * BLK, hd), bf16),
            pltpu.VMEM((hd, TOPK * BLK), bf16),
            pltpu.VMEM((TOPK * BLK, hd), bf16),
            pltpu.VMEM((nb, TOPK + 1, BLK, hd), f32),
            pltpu.VMEM((nb, TOPK + 1, BLK, hd), f32),
            pltpu.VMEM((n * nb, BLK, hd), bf16),
            pltpu.VMEM((n * nb, BLK, hd), bf16),
            dma((3, nb)),
            dma((nb,)),
            dma((2,)),
        ]
        + [dma((n * nb,))] * 8,
        compiler_params=pltpu.CompilerParams(
            collective_id=0, has_side_effects=True, vmem_limit_bytes=63 * 1024 * 1024
        ),
        cost_estimate=pl.CostEstimate(
            flops=pairs * 5 * 2 * rows * BLK * hd,
            bytes_accessed=4 * tokens * heads * hd * 2 + 4 * tokens * hd * 2,
            transcendentals=pairs * rows * BLK,
        ),
    )(
        block_lists,
        queries.reshape(flat),
        keys.reshape(blocks),
        values.reshape(blocks),
        output.reshape(flat),
        d_output.reshape(flat),
    )
    return (
        d_queries.reshape(queries.shape),
        d_keys.reshape(keys.shape),
        d_values.reshape(values.shape),
    )


def solution(mesh):
    return jax.shard_map(
        shards,
        mesh=mesh,
        in_specs=(
            P(("dp", "ctx"), None, None),
            P(("dp", "ctx"), None),
            P(("dp", "ctx"), None),
            P(("dp", "ctx"), None, None),
            P(("dp", "ctx"), None, None),
            P("dp", None),
        ),
        out_specs=(P(("dp", "ctx"), None, None), P(("dp", "ctx"), None), P(("dp", "ctx"), None)),
        check_vma=False,
    )
```

```python
import functools

import jax
import jax.numpy as jnp
from jax import lax
from jax.experimental import pallas as pl
from jax.experimental.pallas import tpu as pltpu
from jax.sharding import PartitionSpec as P

BLK = 256
TOPK = 3
CH = 256
MESH = pl.DeviceIdType.MESH
LOG2E = 1.4426950408889634


def kernel(
    n, nb, heads, hd,
    lists, q_hbm, k_hbm, v_hbm, o_hbm, g_hbm,
    dq_hbm, dk_hbm, dv_hbm,
    q, g, o, qt, gt, delta, top0, sum0, fac0, probs, kfull, vfull, kcat, kcat_t, vcat,
    part_v, part_k, dvbuf, dkbuf, dvslot, dkslot, rank,
    in_sem, out_sem, own_sem,
    k_send, k_recv, v_send, v_recv, dv_send, dv_recv, dk_send, dk_recv,
    dvs_send, dvs_recv, dks_send, dks_recv,
):
    me = lax.axis_index("ctx")
    rows = BLK * heads
    nch = rows // CH
    scaling = hd ** (-0.5)
    last = n - 1
    slots = min((TOPK - 1) * nb, last * nb)

    def up(hbm, full, send, recv, owner, i, own):
        at = owner * nb + i
        return pltpu.make_async_remote_copy(
            src_ref=hbm.at[i] if own else full.at[at],
            dst_ref=full.at[at],
            send_sem=send.at[at],
            recv_sem=recv.at[at],
            device_id={"ctx": me + 1},
            device_id_type=MESH,
        )

    k_up = functools.partial(up, k_hbm, kfull, k_send, k_recv)
    v_up = functools.partial(up, v_hbm, vfull, v_send, v_recv)

    def down(buf, send, recv, at):
        return pltpu.make_async_remote_copy(
            src_ref=buf.at[at],
            dst_ref=buf.at[at],
            send_sem=send.at[at],
            recv_sem=recv.at[at],
            device_id={"ctx": me - 1},
            device_id_type=MESH,
        )

    dv_down = functools.partial(down, dvbuf, dv_send, dv_recv)
    dk_down = functools.partial(down, dkbuf, dk_send, dk_recv)
    dv_slot = functools.partial(down, dvslot, dvs_send, dvs_recv)
    dk_slot = functools.partial(down, dkslot, dks_send, dks_recv)

    def loop(low, high, step):
        def body(i, _):
            step(i)
            return 0

        if low < high:
            lax.fori_loop(low, high, body, 0)

    def in_copy(lb, which):
        src, dst = ((q_hbm, q), (g_hbm, g), (o_hbm, o))[which]
        return pltpu.make_async_copy(src.at[lb], dst.at[lb], in_sem.at[which, lb])

    def dq_copy(lb):
        return pltpu.make_async_copy(o.at[lb], dq_hbm.at[lb], out_sem.at[lb])

    own_k = pltpu.make_async_copy(k_hbm, kfull.at[pl.ds(me * nb, nb)], own_sem.at[0])
    own_v = pltpu.make_async_copy(v_hbm, vfull.at[pl.ds(me * nb, nb)], own_sem.at[1])

    barrier = pltpu.get_barrier_semaphore()

    @pl.when(me > 0)
    def _():
        pl.semaphore_signal(barrier, inc=1, device_id={"ctx": me - 1}, device_id_type=MESH)

    @pl.when(me < last)
    def _():
        pl.semaphore_signal(barrier, inc=1, device_id={"ctx": me + 1}, device_id_type=MESH)

    pl.semaphore_wait(barrier, jnp.where(me > 0, 1, 0) + jnp.where(me < last, 1, 0))

    @pl.when(me < last)
    def _():
        for i in range(nb):
            k_up(me, i, True).start()

    own_k.start()
    for lb in range(nb):
        for which in range(3):
            in_copy(lb, which).start()
    own_v.start()
    own_k.wait()

    def count(block, seen):
        hit = jnp.bool_(False)
        for lb in range(nb):
            for t in range(1, TOPK):
                hit = hit | (lists[t, last * nb + lb] == block)
        rank[block] = jnp.where(hit, seen, -1)
        return seen + jnp.where(hit, 1, 0)

    lax.fori_loop(0, last * nb, count, jnp.int32(0))

    def prep(lb):
        for which in range(3):
            in_copy(lb, which).wait()

        def chunk(ci, _):
            span = pl.ds(ci * CH, CH)
            gc = g[lb, span]
            qc_t = q[lb, span].T
            qt[lb, ci] = qc_t
            gt[lb, ci] = gc.T
            prod = gc.astype(jnp.float32) * o[lb, span].astype(jnp.float32)
            delta[lb, ci] = jnp.sum(prod.T, axis=0, keepdims=True)
            raw = jnp.dot(kfull[me * nb + lb], qc_t, preferred_element_type=jnp.float32)
            key = lax.broadcasted_iota(jnp.int32, (BLK, CH), 0)
            row = lax.broadcasted_iota(jnp.int32, (BLK, CH), 1) + ci * CH
            raw = jnp.where(key * heads <= row, raw, -jnp.inf)
            top = jnp.max(raw, axis=0, keepdims=True)
            e = jnp.exp2((raw - top) * (scaling * LOG2E))
            probs[lb, ci, 0:BLK] = e
            top0[lb, ci] = top
            sum0[lb, ci] = jnp.sum(e, axis=0, keepdims=True)
            return 0

        lax.fori_loop(0, nch, chunk, 0, unroll=2)
        part_v[lb, TOPK] = jnp.zeros((BLK, hd), jnp.float32)
        part_k[lb, TOPK] = jnp.zeros((BLK, hd), jnp.float32)

    def pass_key(j):
        @pl.when(me >= j)
        def _():
            def one(i):
                k_up(me - j, i, False).wait_recv()

                @pl.when(me < last)
                def _():
                    k_up(me - j, i, False).start()

            loop(0, nb, one)

    loop(0, 2, prep)
    pass_key(1)
    loop(2, nb, prep)
    loop(2, n, pass_key)

    @pl.when(me < last)
    def _():
        for i in range(nb):
            v_up(me, i, True).start()

    def pass_value(j):
        @pl.when((me >= j) & (me < last))
        def _():
            def one(i):
                v_up(me - j, i, False).wait_recv()
                v_up(me - j, i, False).start()

            loop(0, nb, one)

    def entry(lb, t):
        return lists[t, me * nb + lb]

    def phase_a(lb):
        for t in range(1, TOPK):
            kcat[t * BLK : (t + 1) * BLK] = kfull[jnp.maximum(entry(lb, t), 0)]
            part_v[lb, t] = jnp.zeros((BLK, hd), jnp.float32)
        listed = [entry(lb, t) >= 0 for t in range(1, TOPK)]

        def chunk(ci, _):
            raw = jnp.dot(kcat[BLK:], qt[lb, ci], preferred_element_type=jnp.float32)
            first = top0[lb, ci]
            top = first
            for t in range(TOPK - 1):
                high = jnp.max(raw[t * BLK : (t + 1) * BLK], axis=0, keepdims=True)
                top = jnp.maximum(top, jnp.where(listed[t], high, -jnp.inf))
            shrink = jnp.exp2((first - top) * (scaling * LOG2E))
            total = sum0[lb, ci] * shrink
            exps = []
            for t in range(TOPK - 1):
                low = jnp.where(listed[t], top, jnp.inf)
                e = jnp.exp2((raw[t * BLK : (t + 1) * BLK] - low) * (scaling * LOG2E))
                total = total + jnp.sum(e, axis=0, keepdims=True)
                exps.append(e)
            inv = 1.0 / total
            fac0[lb, ci] = shrink * inv
            gc = g[lb, pl.ds(ci * CH, CH)]
            for t in range(1, TOPK):
                p = exps[t - 1] * inv
                probs[lb, ci, t * BLK : (t + 1) * BLK] = p
                part_v[lb, t] += jnp.dot(
                    p.astype(jnp.bfloat16), gc, preferred_element_type=jnp.float32
                )
            return 0

        lax.fori_loop(0, nch, chunk, 0, unroll=2)

    def phase_b(lb):
        vcat[0:BLK] = vfull[me * nb + lb]
        for t in range(1, TOPK):
            block = jnp.maximum(entry(lb, t), 0)
            vcat[t * BLK : (t + 1) * BLK] = vfull[block]
        for t in range(TOPK):
            part_k[lb, t] = jnp.zeros((BLK, hd), jnp.float32)
        part_v[lb, 0] = jnp.zeros((BLK, hd), jnp.float32)

        def chunk(ci, _):
            span = pl.ds(ci * CH, CH)
            d_prob = jnp.dot(vcat[...], gt[lb, ci], preferred_element_type=jnp.float32)
            qc = q[lb, span]
            for t in range(TOPK):
                part = slice(t * BLK, (t + 1) * BLK)
                p = probs[lb, ci, part]
                if t == 0:
                    p = p * fac0[lb, ci]
                    part_v[lb, 0] += jnp.dot(
                        p.astype(jnp.bfloat16), g[lb, span], preferred_element_type=jnp.float32
                    )
                ds = (p * (d_prob[part] - delta[lb, ci])).astype(jnp.bfloat16)
                part_k[lb, t] += jnp.dot(ds, qc, preferred_element_type=jnp.float32)
                probs[lb, ci, part] = ds.astype(jnp.float32)
            return 0

        lax.fori_loop(0, nch, chunk, 0, unroll=2)

    def dq_pass(lb):
        kcat[0:BLK] = kfull[me * nb + lb]
        for t in range(1, TOPK):
            kcat[t * BLK : (t + 1) * BLK] = kfull[jnp.maximum(entry(lb, t), 0)]
        kcat_t[...] = kcat[...].T

        def chunk(ci, _):
            ds = probs[lb, ci].astype(jnp.bfloat16)
            dq_t = jnp.dot(kcat_t[...], ds, preferred_element_type=jnp.float32)
            o[lb, pl.ds(ci * CH, CH)] = (dq_t.T * scaling).astype(jnp.bfloat16)
            return 0

        lax.fori_loop(0, nch, chunk, 0, unroll=2)
        dq_copy(lb).start()

    def local_sum(part, block):
        total = None
        for lb in range(nb):
            slot = jnp.int32(TOPK)
            for t in range(TOPK):
                slot = jnp.where(entry(lb, t) == block, t, slot)
            term = part[lb, slot]
            total = term if total is None else total + term
        return total

    def chain(part, buf, copy, slot, slot_copy, factor, owner):
        def one(i):
            at = owner * nb + i

            def put(total):
                buf[at] = (total * jnp.where(owner == me, factor, 1.0)).astype(jnp.bfloat16)

            @pl.when(me < last - 1)
            def _():
                copy(at).wait_recv()
                put(local_sum(part, at) + buf[at].astype(jnp.float32))

            @pl.when(me == last - 1)
            def _():
                @pl.when(at < slots)
                def _():
                    slot_copy(at).wait_recv()

                mine = rank[at]

                def pick(s, total):
                    return total + jnp.where(mine == s, slot[s].astype(jnp.float32), 0.0)

                put(lax.fori_loop(0, jnp.minimum(at + 1, slots), pick, local_sum(part, at)))

            @pl.when(me == last)
            def _():
                put(local_sum(part, at))

            @pl.when((owner < me) & (me < last))
            def _():
                copy(at).start()

        @pl.when(owner <= me)
        def _():
            loop(0, nb, one)

    def send_slots(part, slot, slot_copy):
        def one(s):
            block = lax.fori_loop(
                0, last * nb, lambda b, got: jnp.where(rank[b] == s, b, got), jnp.int32(-2)
            )
            slot[s] = local_sum(part, block).astype(jnp.bfloat16)
            slot_copy(s).start()

        loop(0, slots, one)

    def dv_step(owner):
        chain(part_v, dvbuf, dv_down, dvslot, dv_slot, 1.0, owner)

    def dk_step(owner):
        chain(part_k, dkbuf, dk_down, dkslot, dk_slot, scaling, owner)

    late = nb - 2
    loop(0, late, phase_a)
    pass_value(1)
    loop(late, nb - 1, phase_a)
    if n > 2:
        pass_value(2)
    phase_a(nb - 1)
    loop(3, n, pass_value)

    @pl.when(me == last)
    def _():
        send_slots(part_v, dvslot, dv_slot)

        def arrive(j):
            loop(0, nb, lambda i: v_up(me - j, i, False).wait_recv())

        loop(1, n, arrive)

    own_v.wait()

    half = nb // 2
    loop(0, half, phase_b)

    @pl.when((me > 0) & (me < last))
    def _():
        dv_step(0)

    loop(half, nb, phase_b)

    @pl.when(me == 0)
    def _():
        dv_step(0)

    @pl.when(me < last)
    def _():
        loop(0, nb, dq_pass)

    @pl.when((me > 0) & (me < last))
    def _():
        loop(1, n, dv_step)

    @pl.when(me == last)
    def _():
        send_slots(part_k, dkslot, dk_slot)
        dk_step(last)
        dv_step(last)
        loop(0, nb, dq_pass)

    dv_out = pltpu.make_async_copy(dvbuf.at[pl.ds(me * nb, nb)], dv_hbm, own_sem.at[1])
    dv_out.start()

    @pl.when(me < last)
    def _():
        loop(0, n, dk_step)

    dk_out = pltpu.make_async_copy(dkbuf.at[pl.ds(me * nb, nb)], dk_hbm, own_sem.at[0])
    dk_out.start()
    for lb in range(nb):
        dq_copy(lb).wait()

    def finish_up(j):
        def one(i):
            @pl.when((j <= me) & (me < last))
            def _():
                k_up(j, i, False).wait_send()
                v_up(j, i, False).wait_send()

            @pl.when((j < me) & (me < last))
            def _():
                dv_down(j * nb + i).wait_send()
                dk_down(j * nb + i).wait_send()

            @pl.when((me == last) & (j * nb + i < slots))
            def _():
                dv_slot(j * nb + i).wait_send()
                dk_slot(j * nb + i).wait_send()

        loop(0, nb, one)

    loop(0, n, finish_up)
    dv_out.wait()
    dk_out.wait()


def shards(queries, keys, values, output, d_output, block_lists):
    tokens, heads, hd = queries.shape
    n = lax.axis_size("ctx")
    nb = tokens // BLK
    rows = BLK * heads
    nch = rows // CH
    flat = (nb, rows, hd)
    blocks = (nb, BLK, hd)
    bf16, f32 = jnp.bfloat16, jnp.float32
    dma = pltpu.SemaphoreType.DMA
    any_spec = pl.BlockSpec(memory_space=pl.ANY)
    pairs = nb * TOPK
    slots = min((TOPK - 1) * nb, (n - 1) * nb)
    d_queries, d_keys, d_values = pl.pallas_call(
        functools.partial(kernel, n, nb, heads, hd),
        out_shape=(
            jax.ShapeDtypeStruct(flat, bf16),
            jax.ShapeDtypeStruct(blocks, bf16),
            jax.ShapeDtypeStruct(blocks, bf16),
        ),
        in_specs=[pl.BlockSpec(memory_space=pltpu.SMEM)] + [any_spec] * 5,
        out_specs=(any_spec,) * 3,
        scratch_shapes=[
            pltpu.VMEM(flat, bf16),
            pltpu.VMEM(flat, bf16),
            pltpu.VMEM(flat, bf16),
            pltpu.VMEM((nb, nch, hd, CH), bf16),
            pltpu.VMEM((nb, nch, hd, CH), bf16),
            pltpu.VMEM((nb, nch, 1, CH), f32),
            pltpu.VMEM((nb, nch, 1, CH), f32),
            pltpu.VMEM((nb, nch, 1, CH), f32),
            pltpu.VMEM((nb, nch, 1, CH), f32),
            pltpu.VMEM((nb, nch, TOPK * BLK, CH), f32),
            pltpu.VMEM((n * nb, BLK, hd), bf16),
            pltpu.VMEM((n * nb, BLK, hd), bf16),
            pltpu.VMEM((TOPK * BLK, hd), bf16),
            pltpu.VMEM((hd, TOPK * BLK), bf16),
            pltpu.VMEM((TOPK * BLK, hd), bf16),
            pltpu.VMEM((nb, TOPK + 1, BLK, hd), f32),
            pltpu.VMEM((nb, TOPK + 1, BLK, hd), f32),
            pltpu.VMEM((n * nb, BLK, hd), bf16),
            pltpu.VMEM((n * nb, BLK, hd), bf16),
            pltpu.VMEM((slots, BLK, hd), bf16),
            pltpu.VMEM((slots, BLK, hd), bf16),
            pltpu.SMEM(((n - 1) * nb,), jnp.int32),
            dma((3, nb)),
            dma((nb,)),
            dma((2,)),
        ]
        + [dma((n * nb,))] * 8
        + [dma((slots,))] * 4,
        compiler_params=pltpu.CompilerParams(
            collective_id=0, has_side_effects=True, vmem_limit_bytes=63 * 1024 * 1024
        ),
        cost_estimate=pl.CostEstimate(
            flops=pairs * 5 * 2 * rows * BLK * hd,
            bytes_accessed=4 * tokens * heads * hd * 2 + 4 * tokens * hd * 2,
            transcendentals=pairs * rows * BLK,
        ),
    )(
        block_lists.T,
        queries.reshape(flat),
        keys.reshape(blocks),
        values.reshape(blocks),
        output.reshape(flat),
        d_output.reshape(flat),
    )
    return (
        d_queries.reshape(queries.shape),
        d_keys.reshape(keys.shape),
        d_values.reshape(values.shape),
    )


def solution(mesh):
    return jax.shard_map(
        shards,
        mesh=mesh,
        in_specs=(
            P(("dp", "ctx"), None, None),
            P(("dp", "ctx"), None),
            P(("dp", "ctx"), None),
            P(("dp", "ctx"), None, None),
            P(("dp", "ctx"), None, None),
            P("dp", None),
        ),
        out_specs=(P(("dp", "ctx"), None, None), P(("dp", "ctx"), None), P(("dp", "ctx"), None)),
        check_vma=False,
    )
```

```python
import functools

import jax
import jax.numpy as jnp
from jax import lax
from jax.experimental import pallas as pl
from jax.experimental.pallas import tpu as pltpu
from jax.sharding import PartitionSpec as P

BLK = 256
TOPK = 3
CH = 256
MESH = pl.DeviceIdType.MESH
LOG2E = 1.4426950408889634


def kernel(
    n, nb, heads, hd,
    lists, q_hbm, k_hbm, v_hbm, o_hbm, g_hbm,
    dq_hbm, dk_hbm, dv_hbm,
    q, g, o, qt, gt, delta, top0, sum0, fac0, probs, kfull, vfull, kcat, kcat_t, vcat,
    part_v, part_k, dvbuf, dkbuf, dvslot, dkslot, rank,
    in_sem, out_sem, own_sem,
    k_send, k_recv, v_send, v_recv, dv_send, dv_recv, dk_send, dk_recv,
    dvs_send, dvs_recv, dks_send, dks_recv,
):
    me = lax.axis_index("ctx")
    rows = BLK * heads
    nch = rows // CH
    scaling = hd ** (-0.5)
    last = n - 1
    slots = min((TOPK - 1) * nb, last * nb)

    def up(hbm, full, send, recv, owner, i, own):
        at = owner * nb + i
        return pltpu.make_async_remote_copy(
            src_ref=hbm.at[i] if own else full.at[at],
            dst_ref=full.at[at],
            send_sem=send.at[at],
            recv_sem=recv.at[at],
            device_id={"ctx": me + 1},
            device_id_type=MESH,
        )

    k_up = functools.partial(up, k_hbm, kfull, k_send, k_recv)
    v_up = functools.partial(up, v_hbm, vfull, v_send, v_recv)

    def down(buf, send, recv, at):
        return pltpu.make_async_remote_copy(
            src_ref=buf.at[at],
            dst_ref=buf.at[at],
            send_sem=send.at[at],
            recv_sem=recv.at[at],
            device_id={"ctx": me - 1},
            device_id_type=MESH,
        )

    dv_down = functools.partial(down, dvbuf, dv_send, dv_recv)
    dk_down = functools.partial(down, dkbuf, dk_send, dk_recv)
    dv_slot = functools.partial(down, dvslot, dvs_send, dvs_recv)
    dk_slot = functools.partial(down, dkslot, dks_send, dks_recv)

    def loop(low, high, step):
        def body(i, _):
            step(i)
            return 0

        if low < high:
            lax.fori_loop(low, high, body, 0)

    def in_copy(lb, which):
        src, dst = ((q_hbm, q), (g_hbm, g), (o_hbm, o))[which]
        return pltpu.make_async_copy(src.at[lb], dst.at[lb], in_sem.at[which, lb])

    def dq_copy(lb):
        return pltpu.make_async_copy(o.at[lb], dq_hbm.at[lb], out_sem.at[lb])

    own_k = pltpu.make_async_copy(k_hbm, kfull.at[pl.ds(me * nb, nb)], own_sem.at[0])
    own_v = pltpu.make_async_copy(v_hbm, vfull.at[pl.ds(me * nb, nb)], own_sem.at[1])

    barrier = pltpu.get_barrier_semaphore()

    @pl.when(me > 0)
    def _():
        pl.semaphore_signal(barrier, inc=1, device_id={"ctx": me - 1}, device_id_type=MESH)

    @pl.when(me < last)
    def _():
        pl.semaphore_signal(barrier, inc=1, device_id={"ctx": me + 1}, device_id_type=MESH)

    pl.semaphore_wait(barrier, jnp.where(me > 0, 1, 0) + jnp.where(me < last, 1, 0))

    @pl.when(me < last)
    def _():
        for i in range(nb):
            k_up(me, i, True).start()

    own_k.start()
    for lb in range(nb):
        for which in range(3):
            in_copy(lb, which).start()
    own_v.start()
    own_k.wait()

    def count(block, seen):
        hit = jnp.bool_(False)
        for lb in range(nb):
            for t in range(1, TOPK):
                hit = hit | (lists[t, last * nb + lb] == block)
        rank[block] = jnp.where(hit, seen, -1)
        return seen + jnp.where(hit, 1, 0)

    lax.fori_loop(0, last * nb, count, jnp.int32(0))

    def prep(lb):
        for which in range(3):
            in_copy(lb, which).wait()

        def chunk(ci, _):
            span = pl.ds(ci * CH, CH)
            gc = g[lb, span]
            qc_t = q[lb, span].T
            qt[lb, ci] = qc_t
            gt[lb, ci] = gc.T
            prod = gc.astype(jnp.float32) * o[lb, span].astype(jnp.float32)
            delta[lb, ci] = jnp.sum(prod.T, axis=0, keepdims=True)
            raw = jnp.dot(kfull[me * nb + lb], qc_t, preferred_element_type=jnp.float32)
            key = lax.broadcasted_iota(jnp.int32, (BLK, CH), 0)
            row = lax.broadcasted_iota(jnp.int32, (BLK, CH), 1) + ci * CH
            raw = jnp.where(key * heads <= row, raw, -jnp.inf)
            top = jnp.max(raw, axis=0, keepdims=True)
            e = jnp.exp2((raw - top) * (scaling * LOG2E))
            probs[lb, ci, 0:BLK] = e
            top0[lb, ci] = top
            sum0[lb, ci] = jnp.sum(e, axis=0, keepdims=True)
            return 0

        lax.fori_loop(0, nch, chunk, 0, unroll=2)
        part_v[lb, TOPK] = jnp.zeros((BLK, hd), jnp.float32)
        part_k[lb, TOPK] = jnp.zeros((BLK, hd), jnp.float32)

    def pass_key(j):
        @pl.when(me >= j)
        def _():
            def one(i):
                k_up(me - j, i, False).wait_recv()

                @pl.when(me < last)
                def _():
                    k_up(me - j, i, False).start()

            loop(0, nb, one)

    loop(0, 2, prep)
    pass_key(1)
    loop(2, nb, prep)
    loop(2, n, pass_key)

    @pl.when(me < last)
    def _():
        for i in range(nb):
            v_up(me, i, True).start()

    def pass_value(j):
        @pl.when((me >= j) & (me < last))
        def _():
            def one(i):
                v_up(me - j, i, False).wait_recv()
                v_up(me - j, i, False).start()

            loop(0, nb, one)

    def entry(lb, t):
        return lists[t, me * nb + lb]

    def phase_a(lb):
        for t in range(1, TOPK):
            kcat[t * BLK : (t + 1) * BLK] = kfull[jnp.maximum(entry(lb, t), 0)]
            part_v[lb, t] = jnp.zeros((BLK, hd), jnp.float32)
        listed = [entry(lb, t) >= 0 for t in range(1, TOPK)]

        def chunk(ci, _):
            raw = jnp.dot(kcat[BLK:], qt[lb, ci], preferred_element_type=jnp.float32)
            first = top0[lb, ci]
            top = first
            for t in range(TOPK - 1):
                high = jnp.max(raw[t * BLK : (t + 1) * BLK], axis=0, keepdims=True)
                top = jnp.maximum(top, jnp.where(listed[t], high, -jnp.inf))
            shrink = jnp.exp2((first - top) * (scaling * LOG2E))
            total = sum0[lb, ci] * shrink
            exps = []
            for t in range(TOPK - 1):
                low = jnp.where(listed[t], top, jnp.inf)
                e = jnp.exp2((raw[t * BLK : (t + 1) * BLK] - low) * (scaling * LOG2E))
                total = total + jnp.sum(e, axis=0, keepdims=True)
                exps.append(e)
            inv = 1.0 / total
            fac0[lb, ci] = shrink * inv
            gc = g[lb, pl.ds(ci * CH, CH)]
            for t in range(1, TOPK):
                p = exps[t - 1] * inv
                probs[lb, ci, t * BLK : (t + 1) * BLK] = p
                part_v[lb, t] += jnp.dot(
                    p.astype(jnp.bfloat16), gc, preferred_element_type=jnp.float32
                )
            return 0

        lax.fori_loop(0, nch, chunk, 0, unroll=2)

    def phase_b(lb):
        vcat[0:BLK] = vfull[me * nb + lb]
        for t in range(1, TOPK):
            block = jnp.maximum(entry(lb, t), 0)
            vcat[t * BLK : (t + 1) * BLK] = vfull[block]
        for t in range(TOPK):
            part_k[lb, t] = jnp.zeros((BLK, hd), jnp.float32)
        part_v[lb, 0] = jnp.zeros((BLK, hd), jnp.float32)

        def chunk(ci, _):
            span = pl.ds(ci * CH, CH)
            d_prob = jnp.dot(vcat[...], gt[lb, ci], preferred_element_type=jnp.float32)
            qc = q[lb, span]
            for t in range(TOPK):
                part = slice(t * BLK, (t + 1) * BLK)
                p = probs[lb, ci, part]
                if t == 0:
                    p = p * fac0[lb, ci]
                    part_v[lb, 0] += jnp.dot(
                        p.astype(jnp.bfloat16), g[lb, span], preferred_element_type=jnp.float32
                    )
                ds = (p * (d_prob[part] - delta[lb, ci])).astype(jnp.bfloat16)
                part_k[lb, t] += jnp.dot(ds, qc, preferred_element_type=jnp.float32)
                probs[lb, ci, part] = ds.astype(jnp.float32)
            return 0

        lax.fori_loop(0, nch, chunk, 0, unroll=2)

    def dq_pass(lb):
        kcat[0:BLK] = kfull[me * nb + lb]
        for t in range(1, TOPK):
            kcat[t * BLK : (t + 1) * BLK] = kfull[jnp.maximum(entry(lb, t), 0)]
        kcat_t[...] = kcat[...].T

        def chunk(ci, _):
            ds = probs[lb, ci].astype(jnp.bfloat16)
            dq_t = jnp.dot(kcat_t[...], ds, preferred_element_type=jnp.float32)
            o[lb, pl.ds(ci * CH, CH)] = (dq_t.T * scaling).astype(jnp.bfloat16)
            return 0

        lax.fori_loop(0, nch, chunk, 0, unroll=2)
        dq_copy(lb).start()

    def local_sum(part, block):
        total = None
        for lb in range(nb):
            slot = jnp.int32(TOPK)
            for t in range(TOPK):
                slot = jnp.where(entry(lb, t) == block, t, slot)
            term = part[lb, slot]
            total = term if total is None else total + term
        return total

    def chain(part, buf, copy, slot, slot_copy, factor, owner):
        def one(i):
            at = owner * nb + i

            def put(total):
                buf[at] = (total * jnp.where(owner == me, factor, 1.0)).astype(jnp.bfloat16)

            @pl.when(me < last - 1)
            def _():
                copy(at).wait_recv()
                put(local_sum(part, at) + buf[at].astype(jnp.float32))

            @pl.when(me == last - 1)
            def _():
                @pl.when(at < slots)
                def _():
                    slot_copy(at).wait_recv()

                mine = rank[at]

                def pick(s, total):
                    return total + jnp.where(mine == s, slot[s].astype(jnp.float32), 0.0)

                put(lax.fori_loop(0, jnp.minimum(at + 1, slots), pick, local_sum(part, at)))

            @pl.when(me == last)
            def _():
                put(local_sum(part, at))

            @pl.when((owner < me) & (me < last))
            def _():
                copy(at).start()

        @pl.when(owner <= me)
        def _():
            loop(0, nb, one)

    def send_slots(part, slot, slot_copy):
        def one(s):
            block = lax.fori_loop(
                0, last * nb, lambda b, got: jnp.where(rank[b] == s, b, got), jnp.int32(-2)
            )
            slot[s] = local_sum(part, block).astype(jnp.bfloat16)
            slot_copy(s).start()

        loop(0, slots, one)

    def dv_step(owner):
        chain(part_v, dvbuf, dv_down, dvslot, dv_slot, 1.0, owner)

    def dk_step(owner):
        chain(part_k, dkbuf, dk_down, dkslot, dk_slot, scaling, owner)

    late = nb - 2
    loop(0, late, phase_a)
    pass_value(1)
    loop(late, nb - 1, phase_a)
    if n > 2:
        pass_value(2)
    phase_a(nb - 1)
    loop(3, n, pass_value)

    @pl.when(me == last)
    def _():
        send_slots(part_v, dvslot, dv_slot)

        def arrive(j):
            loop(0, nb, lambda i: v_up(me - j, i, False).wait_recv())

        loop(1, n, arrive)

    own_v.wait()

    half = nb // 2
    loop(0, half, phase_b)

    @pl.when((me > 0) & (me == last - 1))
    def _():
        dv_step(0)

    loop(half, nb, phase_b)

    @pl.when((me > 0) & (me == last - 1))
    def _():
        loop(1, n, dv_step)

    @pl.when(me < last)
    def _():
        loop(0, nb, dq_pass)

    @pl.when((me == 0) | (me < last - 1))
    def _():
        @pl.when(me < last)
        def _():
            loop(0, n, dv_step)

    @pl.when(me == last)
    def _():
        send_slots(part_k, dkslot, dk_slot)
        dk_step(last)
        dv_step(last)
        loop(0, nb, dq_pass)

    dv_out = pltpu.make_async_copy(dvbuf.at[pl.ds(me * nb, nb)], dv_hbm, own_sem.at[1])
    dv_out.start()

    @pl.when(me < last)
    def _():
        loop(0, n, dk_step)

    dk_out = pltpu.make_async_copy(dkbuf.at[pl.ds(me * nb, nb)], dk_hbm, own_sem.at[0])
    dk_out.start()
    for lb in range(nb):
        dq_copy(lb).wait()

    def finish_up(j):
        def one(i):
            @pl.when((j <= me) & (me < last))
            def _():
                k_up(j, i, False).wait_send()
                v_up(j, i, False).wait_send()

            @pl.when((j < me) & (me < last))
            def _():
                dv_down(j * nb + i).wait_send()
                dk_down(j * nb + i).wait_send()

            @pl.when((me == last) & (j * nb + i < slots))
            def _():
                dv_slot(j * nb + i).wait_send()
                dk_slot(j * nb + i).wait_send()

        loop(0, nb, one)

    loop(0, n, finish_up)
    dv_out.wait()
    dk_out.wait()


def shards(queries, keys, values, output, d_output, block_lists):
    tokens, heads, hd = queries.shape
    n = lax.axis_size("ctx")
    nb = tokens // BLK
    rows = BLK * heads
    nch = rows // CH
    flat = (nb, rows, hd)
    blocks = (nb, BLK, hd)
    bf16, f32 = jnp.bfloat16, jnp.float32
    dma = pltpu.SemaphoreType.DMA
    any_spec = pl.BlockSpec(memory_space=pl.ANY)
    pairs = nb * TOPK
    slots = min((TOPK - 1) * nb, (n - 1) * nb)
    d_queries, d_keys, d_values = pl.pallas_call(
        functools.partial(kernel, n, nb, heads, hd),
        out_shape=(
            jax.ShapeDtypeStruct(flat, bf16),
            jax.ShapeDtypeStruct(blocks, bf16),
            jax.ShapeDtypeStruct(blocks, bf16),
        ),
        in_specs=[pl.BlockSpec(memory_space=pltpu.SMEM)] + [any_spec] * 5,
        out_specs=(any_spec,) * 3,
        scratch_shapes=[
            pltpu.VMEM(flat, bf16),
            pltpu.VMEM(flat, bf16),
            pltpu.VMEM(flat, bf16),
            pltpu.VMEM((nb, nch, hd, CH), bf16),
            pltpu.VMEM((nb, nch, hd, CH), bf16),
            pltpu.VMEM((nb, nch, 1, CH), f32),
            pltpu.VMEM((nb, nch, 1, CH), f32),
            pltpu.VMEM((nb, nch, 1, CH), f32),
            pltpu.VMEM((nb, nch, 1, CH), f32),
            pltpu.VMEM((nb, nch, TOPK * BLK, CH), f32),
            pltpu.VMEM((n * nb, BLK, hd), bf16),
            pltpu.VMEM((n * nb, BLK, hd), bf16),
            pltpu.VMEM((TOPK * BLK, hd), bf16),
            pltpu.VMEM((hd, TOPK * BLK), bf16),
            pltpu.VMEM((TOPK * BLK, hd), bf16),
            pltpu.VMEM((nb, TOPK + 1, BLK, hd), f32),
            pltpu.VMEM((nb, TOPK + 1, BLK, hd), f32),
            pltpu.VMEM((n * nb, BLK, hd), bf16),
            pltpu.VMEM((n * nb, BLK, hd), bf16),
            pltpu.VMEM((slots, BLK, hd), bf16),
            pltpu.VMEM((slots, BLK, hd), bf16),
            pltpu.SMEM(((n - 1) * nb,), jnp.int32),
            dma((3, nb)),
            dma((nb,)),
            dma((2,)),
        ]
        + [dma((n * nb,))] * 8
        + [dma((slots,))] * 4,
        compiler_params=pltpu.CompilerParams(
            collective_id=0, has_side_effects=True, vmem_limit_bytes=63 * 1024 * 1024
        ),
        cost_estimate=pl.CostEstimate(
            flops=pairs * 5 * 2 * rows * BLK * hd,
            bytes_accessed=4 * tokens * heads * hd * 2 + 4 * tokens * hd * 2,
            transcendentals=pairs * rows * BLK,
        ),
    )(
        block_lists.T,
        queries.reshape(flat),
        keys.reshape(blocks),
        values.reshape(blocks),
        output.reshape(flat),
        d_output.reshape(flat),
    )
    return (
        d_queries.reshape(queries.shape),
        d_keys.reshape(keys.shape),
        d_values.reshape(values.shape),
    )


def solution(mesh):
    return jax.shard_map(
        shards,
        mesh=mesh,
        in_specs=(
            P(("dp", "ctx"), None, None),
            P(("dp", "ctx"), None),
            P(("dp", "ctx"), None),
            P(("dp", "ctx"), None, None),
            P(("dp", "ctx"), None, None),
            P("dp", None),
        ),
        out_specs=(P(("dp", "ctx"), None, None), P(("dp", "ctx"), None), P(("dp", "ctx"), None)),
        check_vma=False,
    )
```
